32 devices in a mesh: section: 2 (over x), expert: 16 (over z, y, core).
Axes of the slice: x: 2, y: 2, z: 4, core: 2. Of those that a mesh axis runs over, the one named last changes fastest.
Arguments:
- tokens: bfloat16 [2, 2, 1024, 7168], P('section', None, 'expert'), may hold values from -6 to 6
- expert_ids: int32 [2, 2, 1024, 2], P('section', None, 'expert'), may hold values from 0 to 3, all different within a row; in each aligned block of 64 rows (0 to 63, 64 to 127, ..., all dimensions but the last counted through in order) at most 40 rows name the same one
- gate_weights: float32 [2, 2, 1024, 2], P('section', None, 'expert'), may hold values from 0.1 to 1
- w_gate: bfloat16 [2, 16, 7168, 512], P('section', 'expert'), may hold values from -0.0625 to 0.0625
- w_up: bfloat16 [2, 16, 7168, 512], P('section', 'expert'), may hold values from -0.0625 to 0.0625
- w_down: bfloat16 [2, 16, 512, 7168], P('section', 'expert'), may hold values from -0.125 to 0.125
Outputs:
- passed: bfloat16 [2, 2, 1024, 7168], P('section', None, 'expert')
The draws below stay inside these ranges and needn't reach their ends.
Inputs may be any that keep to these rules, and one draw needn't show every extreme that they name: `expert_ids`: in each aligned block of 64 tokens of one micro-batch (the tokens of one device), the 2 experts of a token differ, and no expert is named by more than 40 tokens; some expert is named by exactly 40.
All inputs are finite; a program needn't handle non-finite values.
Results may differ from the reference program's by a relative error of at most 0.0045.
Values may be sent and summed in bfloat16 or wider, within the bound.
A program may use at most 192 MiB of HBM per device.

```python
import math
import jax
import jax.numpy as jnp
import numpy as np
from jax import lax

D = 7168
FF = 2048
SPLIT = 4
TOP = 2
MB = 2
TOK_MB = 64
FF_DEV = 512
EXPERTS = 4
CAP = 40
TOKENS_S = 1024
N_SECTION = 2
N_EXPERT = 16


def levels(stream_key, extent, split, low, largest):
    level, own = 1.0, jax.random.fold_in(stream_key, 6)
    for position, shards_of in split:
        heights = jnp.exp(jax.random.uniform(jax.random.fold_in(own, position), (shards_of,), jnp.float32, low / len(split), largest / len(split)))
        level = level * jnp.repeat(heights, extent[position] // shards_of).reshape([-1 if axis == position else 1 for axis in range(len(extent))])
    return level


def routed_block(stream_key, own, number, rows, amount, top, bound, skew):
    order = jax.random.permutation(stream_key, amount)
    crowded, ordinary = shares(amount, rows * top, bound, skew, True), shares(amount, rows * top, bound, skew, False)
    places = jnp.arange(amount)

    def named(lengths, offset_by):
        used = int((lengths > 0).sum())
        fixed = max(1, used // 4)
        moved = fixed + (places - fixed + offset_by * (used - fixed)) % max(1, amount - fixed)
        return jnp.zeros((amount,), jnp.int32).at[order[jnp.where(places < fixed, places, moved)]].set(jnp.asarray(lengths, jnp.int32))

    lengths = jnp.where(number % 4 == 0, named(crowded, number // 4), named(ordinary, number - number // 4 - 1))
    mixed = jax.random.permutation(jax.random.fold_in(own, 3), amount)
    giver, receiver = mixed[0:amount // 2 * 2:2], mixed[1:amount // 2 * 2:2]
    room = jnp.minimum(lengths[giver] - 1, bound - lengths[receiver]) // 2
    room = jnp.where((giver == order[0]) | (receiver == order[0]) | (lengths[receiver] == 0), 0, jnp.maximum(room, 0))
    moved = jax.random.randint(jax.random.fold_in(own, 4), (amount // 2,), 0, 1 << 20) % (room + 1)
    lengths = lengths.at[giver].add(-moved).at[receiver].add(moved)
    items = jnp.searchsorted(jnp.cumsum(lengths), jnp.arange(rows * top), side="right").astype(jnp.int32)
    grid = items.reshape(top, rows).T
    grid = grid[jax.random.permutation(jax.random.fold_in(own, 1), rows)]
    offset_by = jax.random.randint(jax.random.fold_in(own, 2), (rows, 1), 0, top)
    return jnp.take_along_axis(grid, (jnp.arange(top)[None, :] + offset_by) % top, axis=1)


def shares(number_of, total, reach, skew, full):
    weights = [(1 << 20) // math.isqrt(standing ** skew) + 1 for standing in range(1, number_of + 1)]
    largest = reach if full else min(reach, max(-(-total // number_of), total * weights[0] // sum(weights)))
    least = 1 if total - largest >= number_of - 1 else 0
    given, rest = [largest] + [least] * (number_of - 1), total - largest - least * (number_of - 1)
    while rest > 0:
        free = [i for i in range(1, number_of) if given[i] < largest] or [i for i in range(1, number_of) if given[i] < reach]
        whole, budget = sum([weights[i] for i in free]), rest
        for i in free:
            extra = min(reach - given[i], max(1, budget * weights[i] // whole), rest)
            given[i] = given[i] + extra
            rest = rest - extra
    return np.array(given)


def centred(key, shape, spread, reach, pieces=(), held_as=jnp.bfloat16):
    factor_of = levels(key, shape, pieces, -0.22, 0.18) if pieces else 1.0
    entries = jax.random.normal(key, shape, jnp.float32) * spread * factor_of
    return jnp.minimum(jnp.maximum(entries, -reach), reach).astype(held_as)


def setup_inputs(seed: int = 0) -> dict:
    seeds = jax.random.split(jax.random.key(seed), 7)
    tokens = centred(seeds[0], (N_SECTION, MB, TOKENS_S, D), 1.0, 6.0, ((0, 2), (2, 16)))
    expert_ids_keys = jax.random.split(jax.random.fold_in(seeds[1], 1), N_SECTION * MB * TOKENS_S // TOK_MB)
    expert_ids_turns = jax.random.permutation(jax.random.fold_in(seeds[1], 3), N_SECTION * MB * TOKENS_S // TOK_MB)
    expert_ids = jax.vmap(lambda own, number: routed_block(jax.random.fold_in(seeds[1], 2), own, number, TOK_MB, EXPERTS, TOP, CAP, 2))(expert_ids_keys, expert_ids_turns).reshape((N_SECTION, MB, TOKENS_S, TOP))
    gate_weights = jnp.clip(0.1 + 0.9 * jax.random.uniform(seeds[2], (N_SECTION, MB, TOKENS_S, TOP), jnp.float32) ** levels(seeds[2], (N_SECTION, MB, TOKENS_S, TOP), ((0, 2), (2, 16)), -0.2, 0.2), 0.1, 1.0)
    w_gate = centred(seeds[3], (N_SECTION, N_EXPERT, D, FF_DEV), D ** -0.5, 0.0625, ((0, 2), (1, 16)))
    w_up = centred(seeds[4], (N_SECTION, N_EXPERT, D, FF_DEV), D ** -0.5, 0.0625, ((0, 2), (1, 16)))
    w_down = centred(seeds[5], (N_SECTION, N_EXPERT, FF_DEV, D), FF ** -0.5, 0.125, ((0, 2), (1, 16)))
    return {"tokens": tokens, "expert_ids": expert_ids, "gate_weights": gate_weights, "w_gate": w_gate, "w_up": w_up, "w_down": w_down}


def normalize(values):
    floats = values.astype(jnp.float32)
    inv_rms = lax.rsqrt(lax.optimization_barrier(jnp.mean(floats * floats, axis=-1, keepdims=True)) + 1e-06)
    return (floats * inv_rms).astype(jnp.bfloat16)

def slot_of(routes):
    flat_ids = routes.reshape(-1)
    onehot = (flat_ids[:, None] == jnp.arange(EXPERTS, dtype=jnp.int32)[None, :]).astype(jnp.int32)
    before = jnp.cumsum(onehot, axis=0) - onehot
    return lax.optimization_barrier(jnp.sum(before * onehot, axis=1)).astype(jnp.int32).reshape(routes.shape)

def expert_rows(operands):
    rows_in, gate_all, up_all, down_all = operands
    summed = jnp.zeros((rows_in.shape[0], D), jnp.float32)
    for shard_idx in range(SPLIT):
        gate_act = jnp.dot(rows_in, gate_all[shard_idx], preferred_element_type=jnp.float32)
        up_act = jnp.dot(rows_in, up_all[shard_idx], preferred_element_type=jnp.float32)
        hidden = (jax.nn.silu(gate_act) * up_act).astype(jnp.bfloat16)
        result = jnp.dot(hidden, down_all[shard_idx], preferred_element_type=jnp.float32).astype(jnp.bfloat16)
        summed = summed + result.astype(jnp.float32)
    return summed

def take_rows(block_rows, index_row):
    return block_rows[index_row]

def reference(tokens, expert_ids, gate_weights, w_gate, w_up, w_down):
    results = [None] * N_SECTION
    block_idx = jnp.broadcast_to(jnp.arange(N_EXPERT, dtype=jnp.int32)[:, None, None], (N_EXPERT, TOK_MB, TOP))
    token_idx = jnp.broadcast_to(jnp.arange(TOK_MB, dtype=jnp.int32)[None, :, None], (N_EXPERT, TOK_MB, TOP))
    for section_idx in range(N_SECTION):
        gate_section = w_gate[section_idx].reshape(EXPERTS, SPLIT, D, FF_DEV)
        up_section = w_up[section_idx].reshape(EXPERTS, SPLIT, D, FF_DEV)
        down_section = w_down[section_idx].reshape(EXPERTS, SPLIT, FF_DEV, D)
        section_out = []
        for micro_idx in range(MB):
            block_tok = tokens[section_idx, micro_idx].reshape(N_EXPERT, TOK_MB, D)
            routes = expert_ids[section_idx, micro_idx].reshape(N_EXPERT, TOK_MB, TOP)
            gate_vals = gate_weights[section_idx, micro_idx].reshape(N_EXPERT, TOK_MB, TOP)
            normed = normalize(block_tok)
            slot_idx = jax.vmap(slot_of)(routes)
            target = routes * CAP + slot_idx
            index_table = jnp.full((N_EXPERT, EXPERTS * CAP), TOK_MB, jnp.int32)
            index_table = index_table.at[block_idx, target].set(token_idx)
            padded = jnp.concatenate([normed, jnp.zeros((N_EXPERT, 1, D), jnp.bfloat16)], axis=1)
            gathered = jax.vmap(take_rows)(padded, index_table)
            gathered = gathered.reshape(N_EXPERT, EXPERTS, CAP, D).transpose(1, 0, 2, 3)
            gathered = gathered.reshape(EXPERTS, N_EXPERT * CAP, D)
            combined = lax.map(expert_rows, (gathered, gate_section, up_section, down_section))
            combined = combined.reshape(EXPERTS, N_EXPERT, CAP, D)
            picked = combined[routes, block_idx, slot_idx]
            mixed_out = block_tok.astype(jnp.float32) + lax.optimization_barrier(jnp.sum(gate_vals[..., None] * picked, axis=2))
            section_out.append(mixed_out.astype(jnp.bfloat16).reshape(TOKENS_S, D))
        results[(section_idx + 1) % N_SECTION] = jnp.stack(section_out, axis=0)
    return jnp.stack(results, axis=0)
```

```python
import functools

import jax
import jax.numpy as jnp
from jax import lax
from jax.experimental import pallas as pl
from jax.experimental.pallas import tpu as pltpu
from jax.sharding import PartitionSpec as P

SPLIT = 4
MESH = pl.DeviceIdType.MESH
VMEM_LIMIT = 60 * 1024 * 1024
Z_AHEAD = 2
Y_AHEAD = 2


def chunk_width(features):
    return max(w for w in range(128, 1025, 128) if features % w == 0)


def normalize(values):
    floats = values.astype(jnp.float32)
    inv_rms = lax.rsqrt(jnp.mean(floats * floats, axis=-1, keepdims=True) + 1e-06)
    return (floats * inv_rms).astype(jnp.bfloat16)


def places(experts):
    me = lax.axis_index("expert")
    own = lax.div(me, SPLIT)
    share = lax.rem(me, SPLIT)
    core = lax.rem(share, 2)
    chip = lax.div(share, 2)
    sibling = own * SPLIT + chip * 2 + (1 - core)
    across = own * SPLIT + (1 - chip) * 2 + core
    others = []
    for step in range(1, experts):
        other = lax.rem(own + step, experts)
        others.append((other, other * SPLIT + share))
    return own, core, chip, sibling, across, others


def remote(src, dst, send, recv, **where):
    return pltpu.make_async_remote_copy(
        src_ref=src, dst_ref=dst, send_sem=send, recv_sem=recv,
        device_id=where, device_id_type=MESH,
    )


def dispatch_kernel(
    experts, chunks, width,
    sel, normed, gate_hbm, up_hbm, hid,
    picked, rows, gate_w, up_w, gate_acc, up_acc,
    w_sem, z_s, z_r, y_s, y_r, a_s, a_r, b_s, b_r,
):
    own, core, chip, sibling, across, others = places(experts)
    units = sel.shape[0] // experts
    load_gate = pltpu.make_async_copy(gate_hbm, gate_w, w_sem.at[0])
    load_up = pltpu.make_async_copy(up_hbm, up_w, w_sem.at[1])
    load_gate.start()
    load_up.start()

    barrier = pltpu.get_barrier_semaphore()
    for partner in [sibling, across] + [dev for _, dev in others]:
        pl.semaphore_signal(barrier, inc=1, device_id={"expert": partner}, device_id_type=MESH)
    pl.semaphore_wait(barrier, experts + 1)

    gate_acc[...] = jnp.zeros_like(gate_acc)
    up_acc[...] = jnp.zeros_like(up_acc)

    def z_copy(c, n):
        other, dev = others[n]
        return remote(picked.at[c, other], rows.at[c, core, chip, own], z_s.at[c, n], z_r.at[c, n], expert=dev)

    def y_copy(c):
        slab = rows.at[c, core, chip]
        return remote(slab, slab, y_s.at[c], y_r.at[c], expert=across)

    def a_copy(c):
        slab = rows.at[c, core, chip]
        return remote(slab, slab, a_s.at[c], a_r.at[c], expert=sibling)

    def b_copy(c):
        slab = rows.at[c, core, 1 - chip]
        return remote(slab, slab, b_s.at[c], b_r.at[c], expert=sibling)

    def multiply(c, co, yo):
        lhs = rows[c, co, yo].reshape(experts * units, width)
        at = pl.ds(pl.multiple_of(c * width, width), width)
        gate_acc[co, yo] += jnp.dot(lhs, gate_w[at, :], preferred_element_type=jnp.float32)
        up_acc[co, yo] += jnp.dot(lhs, up_w[at, :], preferred_element_type=jnp.float32)

    @pl.loop(0, chunks + Z_AHEAD + Y_AHEAD + 1)
    def _(t):
        @pl.when(t < chunks)
        def _():
            at = pl.ds(pl.multiple_of(t * width, width), width)
            block = jnp.dot(sel[...], normed[:, at], preferred_element_type=jnp.float32)
            picked[t] = block.astype(jnp.bfloat16).reshape(experts, units, width)
            for n in range(experts - 1):
                z_copy(t, n).start()
            rows[t, core, chip, own] = picked[t, own]

        c1 = t - Z_AHEAD

        @pl.when((c1 >= 0) & (c1 < chunks))
        def _():
            for n in range(experts - 1):
                z_copy(c1, n).wait_recv()
            y_copy(c1).start()
            a_copy(c1).start()

        c2 = c1 - Y_AHEAD

        @pl.when((c2 >= 0) & (c2 < chunks))
        def _():
            y_copy(c2).wait_recv()
            b_copy(c2).start()

        @pl.when(c2 == 0)
        def _():
            load_gate.wait()
            load_up.wait()

        @pl.when((c2 >= 0) & (c2 < chunks))
        def _():
            @pl.loop(0, 2)
            def _(yo):
                multiply(c2, core, yo)

        c3 = c2 - 1

        @pl.when((c3 >= 0) & (c3 < chunks))
        def _():
            a_copy(c3).wait_recv()
            b_copy(c3).wait_recv()

            @pl.loop(0, 2)
            def _(yo):
                multiply(c3, 1 - core, yo)

    @pl.loop(0, chunks)
    def _(c):
        for n in range(experts - 1):
            z_copy(c, n).wait_send()
        y_copy(c).wait_send()
        a_copy(c).wait_send()
        b_copy(c).wait_send()

    @pl.loop(0, 4)
    def _(k):
        co, yo = lax.div(k, 2), lax.rem(k, 2)
        gate = gate_acc[co, yo]
        hid[co, yo] = (gate / (1.0 + jnp.exp(-gate)) * up_acc[co, yo]).astype(jnp.bfloat16)


def return_kernel(
    experts, chunks, width,
    hid, down_hbm, mix_hi, mix_lo, tok, out,
    part, from_core, from_chip, back, staged, down_w,
    w_sem, a_s, a_r, y_s, y_r, z_s, z_r, o_s, o_r,
):
    own, core, chip, sibling, across, others = places(experts)
    units = back.shape[2]
    section = lax.axis_index("section")
    n_sections = lax.axis_size("section")
    after = lax.rem(section + 1, n_sections)
    before = lax.rem(section + n_sections - 1, n_sections)
    load = pltpu.make_async_copy(down_hbm, down_w, w_sem.at[0])
    load.start()

    barrier = pltpu.get_barrier_semaphore()
    for partner in [sibling, across] + [dev for _, dev in others]:
        pl.semaphore_signal(barrier, inc=1, device_id={"expert": partner}, device_id_type=MESH)
    pl.semaphore_signal(barrier, inc=1, device_id={"section": before}, device_id_type=MESH)
    pl.semaphore_wait(barrier, experts + 2)
    load.wait()

    def columns(c):
        return pl.ds(pl.multiple_of(c * width, width), width)

    def a_copy(c):
        return remote(part.at[c, 1 - core], from_core.at[c], a_s.at[c], a_r.at[c], expert=sibling)

    def y_copy(c):
        return remote(part.at[c, core, 1 - chip], from_chip.at[c], y_s.at[c], y_r.at[c], expert=across)

    def z_copy(c, n):
        other, dev = others[n]
        return remote(part.at[c, core, chip, other], back.at[c, own], z_s.at[c, n], z_r.at[c, n], expert=dev)

    def o_copy(c):
        return remote(staged.at[c], out.at[:, columns(c)], o_s.at[c], o_r.at[c], section=after)

    def multiply(c, co, yo):
        block = jnp.dot(hid[co, yo].reshape(experts * units, hid.shape[-1]), down_w[:, columns(c)], preferred_element_type=jnp.float32)
        part[c, co, yo] = block.astype(jnp.bfloat16).reshape(experts, units, width)

    @pl.loop(0, chunks + 2 + Y_AHEAD + Z_AHEAD)
    def _(t):
        @pl.when(t < chunks)
        def _():
            @pl.loop(0, 2)
            def _(yo):
                multiply(t, 1 - core, yo)

            a_copy(t).start()

            @pl.loop(0, 2)
            def _(yo):
                multiply(t, core, yo)

        c1 = t - 1

        @pl.when((c1 >= 0) & (c1 < chunks))
        def _():
            a_copy(c1).wait_recv()

            @pl.loop(0, experts)
            def _(e):
                total = part[c1, core, 1 - chip, e].astype(jnp.float32) + from_core[c1, 1 - chip, e].astype(jnp.float32)
                part[c1, core, 1 - chip, e] = total.astype(jnp.bfloat16)

            y_copy(c1).start()

        c2 = c1 - Y_AHEAD

        @pl.when((c2 >= 0) & (c2 < chunks))
        def _():
            y_copy(c2).wait_recv()

            @pl.loop(0, experts)
            def _(e):
                total = part[c2, core, chip, e].astype(jnp.float32) + from_core[c2, chip, e].astype(jnp.float32)
                total = total + from_chip[c2, e].astype(jnp.float32)
                part[c2, core, chip, e] = total.astype(jnp.bfloat16)

            for n in range(experts - 1):
                z_copy(c2, n).start()
            back[c2, own] = part[c2, core, chip, own]

        c3 = c2 - Z_AHEAD

        @pl.when((c3 >= 0) & (c3 < chunks))
        def _():
            for n in range(experts - 1):
                z_copy(c3, n).wait_recv()
            terms = back[c3].reshape(experts * units, width)
            total = jnp.dot(mix_hi[...], terms, preferred_element_type=jnp.float32)
            total += jnp.dot(mix_lo[...], terms, preferred_element_type=jnp.float32)
            total += tok[:, columns(c3)].astype(jnp.float32)
            staged[c3] = total.astype(jnp.bfloat16)
            o_copy(c3).start()

    @pl.loop(0, chunks)
    def _(c):
        a_copy(c).wait_send()
        y_copy(c).wait_send()
        for n in range(experts - 1):
            z_copy(c, n).wait_send()
        o_copy(c).wait()


def local(tokens, expert_ids, gate_weights, w_gate, w_up, w_down):
    n_dev = lax.axis_size("expert")
    experts = n_dev // SPLIT
    local_tok = tokens[0]
    micro_count, tok_rows, features = local_tok.shape
    top_k = expert_ids.shape[-1]
    hidden = w_gate.shape[-1]
    capacity = min(tok_rows, tok_rows * top_k * 5 // (4 * experts))
    units = -(-micro_count * capacity // 16) * 16
    width = chunk_width(features)
    chunks = features // width
    all_tok = micro_count * tok_rows

    ids = expert_ids[0].reshape(micro_count, tok_rows * top_k)
    order = jnp.arange(tok_rows * top_k, dtype=jnp.int32)
    same = (ids[:, :, None] == ids[:, None, :]) & (order[None, :] < order[:, None])[None]
    slot = jnp.sum(same.astype(jnp.int32), axis=2)
    micro = jnp.arange(micro_count, dtype=jnp.int32)[:, None]
    target = (ids * units + micro * capacity + slot).reshape(all_tok, top_k)
    positions = jnp.arange(experts * units, dtype=jnp.int32)
    sel = jnp.sum((positions[:, None, None] == target[None]).astype(jnp.float32), axis=2).astype(jnp.bfloat16)
    gates = gate_weights[0].reshape(all_tok, top_k)
    mix = jnp.sum(jnp.where(target[:, :, None] == positions[None, None, :], gates[:, :, None], 0.0), axis=1)
    mix_hi = lax.reduce_precision(mix, 8, 7)
    mix_lo = (mix - mix_hi).astype(jnp.bfloat16)
    mix_hi = mix_hi.astype(jnp.bfloat16)

    flat_tok = local_tok.reshape(all_tok, features)
    normed = normalize(flat_tok)

    vmem = pl.BlockSpec(memory_space=pltpu.VMEM)
    anywhere = pl.BlockSpec(memory_space=pl.ANY)
    dma = pltpu.SemaphoreType.DMA
    bf16 = jnp.bfloat16
    macs = n_dev * units * features * hidden
    hid = pl.pallas_call(
        functools.partial(dispatch_kernel, experts, chunks, width),
        out_shape=jax.ShapeDtypeStruct((2, 2, experts * units, hidden), bf16),
        in_specs=[vmem, vmem, anywhere, anywhere],
        out_specs=vmem,
        scratch_shapes=[
            pltpu.VMEM((chunks, experts, units, width), bf16),
            pltpu.VMEM((chunks, 2, 2, experts, units, width), bf16),
            pltpu.VMEM((features, hidden), bf16),
            pltpu.VMEM((features, hidden), bf16),
            pltpu.VMEM((2, 2, experts * units, hidden), jnp.float32),
            pltpu.VMEM((2, 2, experts * units, hidden), jnp.float32),
            dma((2,)),
            dma((chunks, experts - 1)), dma((chunks, experts - 1)),
            dma((chunks,)), dma((chunks,)),
            dma((chunks,)), dma((chunks,)),
            dma((chunks,)), dma((chunks,)),
        ],
        compiler_params=pltpu.CompilerParams(
            collective_id=0, has_side_effects=True, vmem_limit_bytes=VMEM_LIMIT
        ),
        cost_estimate=pl.CostEstimate(flops=4 * macs, bytes_accessed=4 * features * hidden, transcendentals=0),
        name="dispatch",
    )(sel, normed, w_gate[0, 0], w_up[0, 0])
    passed = pl.pallas_call(
        functools.partial(return_kernel, experts, chunks, width),
        out_shape=jax.ShapeDtypeStruct((all_tok, features), bf16),
        in_specs=[vmem, anywhere, vmem, vmem, vmem],
        out_specs=anywhere,
        scratch_shapes=[
            pltpu.VMEM((chunks, 2, 2, experts, units, width), bf16),
            pltpu.VMEM((chunks, 2, experts, units, width), bf16),
            pltpu.VMEM((chunks, experts, units, width), bf16),
            pltpu.VMEM((chunks, experts, units, width), bf16),
            pltpu.VMEM((chunks, all_tok, width), bf16),
            pltpu.VMEM((hidden, features), bf16),
            dma((1,)),
            dma((chunks,)), dma((chunks,)),
            dma((chunks,)), dma((chunks,)),
            dma((chunks, experts - 1)), dma((chunks, experts - 1)),
            dma((chunks,)), dma((chunks,)),
        ],
        compiler_params=pltpu.CompilerParams(
            collective_id=1, has_side_effects=True, vmem_limit_bytes=VMEM_LIMIT
        ),
        cost_estimate=pl.CostEstimate(flops=2 * macs, bytes_accessed=2 * features * hidden, transcendentals=0),
        name="combine",
    )(hid, w_down[0, 0], mix_hi, mix_lo, flat_tok)
    return passed.reshape(1, micro_count, tok_rows, features)


def solution(mesh):
    return jax.shard_map(
        local,
        mesh=mesh,
        in_specs=(
            P("section", None, "expert", None),
            P("section", None, "expert", None),
            P("section", None, "expert", None),
            P("section", "expert", None, None),
            P("section", "expert", None, None),
            P("section", "expert", None, None),
        ),
        out_specs=P("section", None, "expert", None),
        check_vma=False,
    )
```

```python
import functools

import jax
import jax.numpy as jnp
from jax import lax
from jax.experimental import pallas as pl
from jax.experimental.pallas import tpu as pltpu
from jax.sharding import PartitionSpec as P

SPLIT = 4
MESH = pl.DeviceIdType.MESH
VMEM_LIMIT = 60 * 1024 * 1024
Z_AHEAD = 2
Y_AHEAD = 2
OWN_LATER = 2


def chunk_width(features):
    return max(w for w in range(128, 257, 128) if features % w == 0)


def places(experts):
    me = lax.axis_index("expert")
    own = lax.div(me, SPLIT)
    share = lax.rem(me, SPLIT)
    core = lax.rem(share, 2)
    chip = lax.div(share, 2)
    sibling = own * SPLIT + chip * 2 + (1 - core)
    across = own * SPLIT + (1 - chip) * 2 + core
    others = []
    for step in range(1, experts):
        other = lax.rem(own + step, experts)
        others.append((other, other * SPLIT + share))
    return own, core, chip, sibling, across, others


def remote(src, dst, send, recv, **where):
    return pltpu.make_async_remote_copy(
        src_ref=src, dst_ref=dst, send_sem=send, recv_sem=recv,
        device_id=where, device_id_type=MESH,
    )


def dispatch_kernel(
    experts, chunks, width,
    target, tok, gate_hbm, up_hbm, hid,
    sel, inv_rms, picked, rows, gate_w, up_w, gate_acc, up_acc,
    w_sem, z_s, z_r, y_s, y_r, a_s, a_r, b_s, b_r,
):
    own, core, chip, sibling, across, others = places(experts)
    units = sel.shape[0] // experts

    def columns(c):
        return pl.ds(pl.multiple_of(c * width, width), width)

    load_gate = pltpu.make_async_copy(gate_hbm, gate_w, w_sem.at[0])
    load_up = pltpu.make_async_copy(up_hbm, up_w, w_sem.at[1])
    load_gate.start()
    load_up.start()

    barrier = pltpu.get_barrier_semaphore()
    for partner in [sibling, across] + [dev for _, dev in others]:
        pl.semaphore_signal(barrier, inc=1, device_id={"expert": partner}, device_id_type=MESH)

    places_in = lax.broadcasted_iota(jnp.int32, sel.shape, 0)
    hits = jnp.zeros(sel.shape, jnp.float32)
    for k in range(target.shape[0]):
        hits += jnp.where(places_in == target[k : k + 1, :], 1.0, 0.0)
    sel[...] = hits.astype(jnp.bfloat16)

    def add_squares(c, total):
        part = tok[:, columns(c)].astype(jnp.float32)
        return total + jnp.sum(part * part, axis=1, keepdims=True)

    squares = lax.fori_loop(0, chunks, add_squares, jnp.zeros((tok.shape[0], 1), jnp.float32))
    mean = squares / (chunks * width)
    inv_rms[...] = jnp.broadcast_to(lax.rsqrt(mean + 1e-06), inv_rms.shape)

    pl.semaphore_wait(barrier, experts + 1)
    gate_acc[...] = jnp.zeros_like(gate_acc)
    up_acc[...] = jnp.zeros_like(up_acc)

    def z_copy(c, n):
        other, dev = others[n]
        return remote(picked.at[c, other], rows.at[c, core, chip, own], z_s.at[c, n], z_r.at[c, n], expert=dev)

    def y_copy(c, n):
        home = own if n == experts - 1 else others[experts - 2 - n][0]
        block = rows.at[c, core, chip, home]
        return remote(block, block, y_s.at[c, n], y_r.at[c, n], expert=across)

    def a_copy(c):
        slab = rows.at[c, core, chip]
        return remote(slab, slab, a_s.at[c], a_r.at[c], expert=sibling)

    def b_copy(c):
        slab = rows.at[c, core, 1 - chip]
        return remote(slab, slab, b_s.at[c], b_r.at[c], expert=sibling)

    def multiply(c, co, yo):
        lhs = rows[c, co, yo].reshape(experts * units, width)
        gate_acc[co, yo] += jnp.dot(lhs, gate_w[columns(c), :], preferred_element_type=jnp.float32)
        up_acc[co, yo] += jnp.dot(lhs, up_w[columns(c), :], preferred_element_type=jnp.float32)

    @pl.loop(0, chunks + Z_AHEAD + Y_AHEAD + 1)
    def _(t):
        @pl.when(t < chunks)
        def _():
            normed = (tok[:, columns(t)].astype(jnp.float32) * inv_rms[:, :1]).astype(jnp.bfloat16)
            block = jnp.dot(sel[...], normed, preferred_element_type=jnp.float32)
            picked[t] = block.astype(jnp.bfloat16).reshape(experts, units, width)
            for n in range(experts - 1):
                z_copy(t, n).start()
            rows[t, core, chip, own] = picked[t, own]
            y_copy(t, experts - 1).start()

        c1 = t - Z_AHEAD

        @pl.when((c1 >= 0) & (c1 < chunks))
        def _():
            for n in range(experts - 1):
                z_copy(c1, n).wait_recv()
                y_copy(c1, n).start()
            a_copy(c1).start()

        c2 = c1 - Y_AHEAD

        @pl.when((c2 >= 0) & (c2 < chunks))
        def _():
            for n in range(experts):
                y_copy(c2, n).wait_recv()
            b_copy(c2).start()

        @pl.when(c2 == 0)
        def _():
            load_gate.wait()
            load_up.wait()

        @pl.when((c2 >= 0) & (c2 < chunks))
        def _():
            @pl.loop(0, 2)
            def _(yo):
                multiply(c2, core, yo)

        c3 = c2 - 1

        @pl.when((c3 >= 0) & (c3 < chunks))
        def _():
            a_copy(c3).wait_recv()
            b_copy(c3).wait_recv()

            @pl.loop(0, 2)
            def _(yo):
                multiply(c3, 1 - core, yo)

    @pl.loop(0, chunks)
    def _(c):
        for n in range(experts - 1):
            z_copy(c, n).wait_send()
        for n in range(experts):
            y_copy(c, n).wait_send()
        a_copy(c).wait_send()
        b_copy(c).wait_send()

    @pl.loop(0, 4)
    def _(k):
        co, yo = lax.div(k, 2), lax.rem(k, 2)
        gate = gate_acc[co, yo]
        hid[co, yo] = (gate / (1.0 + jnp.exp(-gate)) * up_acc[co, yo]).astype(jnp.bfloat16)


def return_kernel(
    experts, chunks, width,
    hid, down_hbm, target, gates, tok, out,
    mix_hi, mix_lo, part, from_core, from_chip, back, staged, down_w,
    w_sem, a_s, a_r, y_s, y_r, z_s, z_r, o_s, o_r,
):
    own, core, chip, sibling, across, others = places(experts)
    units = back.shape[2]
    section = lax.axis_index("section")
    n_sections = lax.axis_size("section")
    after = lax.rem(section + 1, n_sections)
    before = lax.rem(section + n_sections - 1, n_sections)

    def columns(c):
        return pl.ds(pl.multiple_of(c * width, width), width)

    def load(c):
        return pltpu.make_async_copy(down_hbm.at[:, columns(c)], down_w.at[:, columns(c)], w_sem.at[c])

    @pl.loop(0, chunks)
    def _(c):
        load(c).start()

    barrier = pltpu.get_barrier_semaphore()
    for partner in [sibling, across] + [dev for _, dev in others]:
        pl.semaphore_signal(barrier, inc=1, device_id={"expert": partner}, device_id_type=MESH)
    pl.semaphore_signal(barrier, inc=1, device_id={"section": before}, device_id_type=MESH)

    places_in = lax.broadcasted_iota(jnp.int32, mix_hi.shape, 1)
    mix = jnp.zeros(mix_hi.shape, jnp.float32)
    for k in range(target.shape[1]):
        mix += jnp.where(places_in == target[:, k : k + 1], gates[:, k : k + 1], 0.0)
    high = mix.astype(jnp.bfloat16)
    mix_hi[...] = high
    mix_lo[...] = (mix - high.astype(jnp.float32)).astype(jnp.bfloat16)

    pl.semaphore_wait(barrier, experts + 2)

    def a_copy(c):
        return remote(part.at[c, 1 - core], from_core.at[c], a_s.at[c], a_r.at[c], expert=sibling)

    def y_copy(c, n):
        home = own if n == experts - 1 else others[n][0]
        return remote(part.at[c, core, 1 - chip, home], from_chip.at[c, home], y_s.at[c, n], y_r.at[c, n], expert=across)

    def whole(c, home):
        total = part[c, core, chip, home].astype(jnp.float32) + from_core[c, chip, home].astype(jnp.float32)
        return (total + from_chip[c, home].astype(jnp.float32)).astype(jnp.bfloat16)

    def z_copy(c, n):
        other, dev = others[n]
        return remote(part.at[c, core, chip, other], back.at[c, own], z_s.at[c, n], z_r.at[c, n], expert=dev)

    def o_copy(c):
        return remote(staged.at[c], out.at[:, columns(c)], o_s.at[c], o_r.at[c], section=after)

    def multiply(c, co, yo):
        block = jnp.dot(hid[co, yo].reshape(experts * units, hid.shape[-1]), down_w[:, columns(c)], preferred_element_type=jnp.float32)
        part[c, co, yo] = block.astype(jnp.bfloat16).reshape(experts, units, width)

    @pl.loop(0, chunks + 2 + Y_AHEAD + Z_AHEAD)
    def _(t):
        @pl.when(t < chunks)
        def _():
            load(t).wait()

            @pl.loop(0, 2)
            def _(yo):
                multiply(t, 1 - core, yo)

            a_copy(t).start()

            @pl.loop(0, 2)
            def _(yo):
                multiply(t, core, yo)

        c1 = t - 1

        @pl.when((c1 >= 0) & (c1 < chunks))
        def _():
            a_copy(c1).wait_recv()

            @pl.loop(0, experts)
            def _(e):
                total = part[c1, core, 1 - chip, e].astype(jnp.float32) + from_core[c1, 1 - chip, e].astype(jnp.float32)
                part[c1, core, 1 - chip, e] = total.astype(jnp.bfloat16)

            for n in range(experts - 1):
                y_copy(c1, n).start()

        late = c1 - OWN_LATER

        @pl.when((late >= 0) & (late < chunks))
        def _():
            y_copy(late, experts - 1).start()

        c2 = c1 - Y_AHEAD

        @pl.when((c2 >= 0) & (c2 < chunks))
        def _():
            for n in range(experts - 1):
                y_copy(c2, n).wait_recv()
                other = others[n][0]
                part[c2, core, chip, other] = whole(c2, other)
                z_copy(c2, n).start()

        c3 = c2 - Z_AHEAD

        @pl.when((c3 >= 0) & (c3 < chunks))
        def _():
            y_copy(c3, experts - 1).wait_recv()
            back[c3, own] = whole(c3, own)
            for n in range(experts - 1):
                z_copy(c3, n).wait_recv()
            terms = back[c3].reshape(experts * units, width)
            total = jnp.dot(mix_hi[...], terms, preferred_element_type=jnp.float32)
            total += jnp.dot(mix_lo[...], terms, preferred_element_type=jnp.float32)
            total += tok[:, columns(c3)].astype(jnp.float32)
            staged[c3] = total.astype(jnp.bfloat16)
            o_copy(c3).start()

    @pl.loop(0, chunks)
    def _(c):
        a_copy(c).wait_send()
        for n in range(experts):
            y_copy(c, n).wait_send()
        for n in range(experts - 1):
            z_copy(c, n).wait_send()
        o_copy(c).wait()


def local(tokens, expert_ids, gate_weights, w_gate, w_up, w_down):
    n_dev = lax.axis_size("expert")
    experts = n_dev // SPLIT
    local_tok = tokens[0]
    micro_count, tok_rows, features = local_tok.shape
    top_k = expert_ids.shape[-1]
    hidden = w_gate.shape[-1]
    capacity = min(tok_rows, tok_rows * top_k * 5 // (4 * experts))
    units = -(-micro_count * capacity // 16) * 16
    width = chunk_width(features)
    chunks = features // width
    all_tok = micro_count * tok_rows

    ids = expert_ids[0].reshape(micro_count, tok_rows * top_k)
    order = jnp.arange(tok_rows * top_k, dtype=jnp.int32)
    same = (ids[:, :, None] == ids[:, None, :]) & (order[None, :] < order[:, None])[None]
    slot = jnp.sum(same.astype(jnp.int32), axis=2)
    micro = jnp.arange(micro_count, dtype=jnp.int32)[:, None]
    target = (ids * units + micro * capacity + slot).reshape(all_tok, top_k)
    gates = gate_weights[0].reshape(all_tok, top_k)
    flat_tok = local_tok.reshape(all_tok, features)

    vmem = pl.BlockSpec(memory_space=pltpu.VMEM)
    anywhere = pl.BlockSpec(memory_space=pl.ANY)
    dma = pltpu.SemaphoreType.DMA
    bf16 = jnp.bfloat16
    macs = n_dev * units * features * hidden
    hid = pl.pallas_call(
        functools.partial(dispatch_kernel, experts, chunks, width),
        out_shape=jax.ShapeDtypeStruct((2, 2, experts * units, hidden), bf16),
        in_specs=[vmem, vmem, anywhere, anywhere],
        out_specs=vmem,
        scratch_shapes=[
            pltpu.VMEM((experts * units, all_tok), bf16),
            pltpu.VMEM((all_tok, 128), jnp.float32),
            pltpu.VMEM((chunks, experts, units, width), bf16),
            pltpu.VMEM((chunks, 2, 2, experts, units, width), bf16),
            pltpu.VMEM((features, hidden), bf16),
            pltpu.VMEM((features, hidden), bf16),
            pltpu.VMEM((2, 2, experts * units, hidden), jnp.float32),
            pltpu.VMEM((2, 2, experts * units, hidden), jnp.float32),
            dma((2,)),
            dma((chunks, experts - 1)), dma((chunks, experts - 1)),
            dma((chunks, experts)), dma((chunks, experts)),
            dma((chunks,)), dma((chunks,)),
            dma((chunks,)), dma((chunks,)),
        ],
        compiler_params=pltpu.CompilerParams(
            collective_id=0, has_side_effects=True, vmem_limit_bytes=VMEM_LIMIT
        ),
        cost_estimate=pl.CostEstimate(flops=4 * macs, bytes_accessed=4 * features * hidden, transcendentals=0),
        name="dispatch",
    )(target.T, flat_tok, w_gate[0, 0], w_up[0, 0])
    passed = pl.pallas_call(
        functools.partial(return_kernel, experts, chunks, width),
        out_shape=jax.ShapeDtypeStruct((all_tok, features), bf16),
        in_specs=[vmem, anywhere, vmem, vmem, vmem],
        out_specs=anywhere,
        scratch_shapes=[
            pltpu.VMEM((all_tok, experts * units), bf16),
            pltpu.VMEM((all_tok, experts * units), bf16),
            pltpu.VMEM((chunks, 2, 2, experts, units, width), bf16),
            pltpu.VMEM((chunks, 2, experts, units, width), bf16),
            pltpu.VMEM((chunks, experts, units, width), bf16),
            pltpu.VMEM((chunks, experts, units, width), bf16),
            pltpu.VMEM((chunks, all_tok, width), bf16),
            pltpu.VMEM((hidden, features), bf16),
            dma((chunks,)),
            dma((chunks,)), dma((chunks,)),
            dma((chunks, experts)), dma((chunks, experts)),
            dma((chunks, experts - 1)), dma((chunks, experts - 1)),
            dma((chunks,)), dma((chunks,)),
        ],
        compiler_params=pltpu.CompilerParams(
            collective_id=1, has_side_effects=True, vmem_limit_bytes=VMEM_LIMIT
        ),
        cost_estimate=pl.CostEstimate(flops=2 * macs, bytes_accessed=2 * features * hidden, transcendentals=0),
        name="combine",
    )(hid, w_down[0, 0], target, gates, flat_tok)
    return passed.reshape(1, micro_count, tok_rows, features)


def solution(mesh):
    return jax.shard_map(
        local,
        mesh=mesh,
        in_specs=(
            P("section", None, "expert", None),
            P("section", None, "expert", None),
            P("section", None, "expert", None),
            P("section", "expert", None, None),
            P("section", "expert", None, None),
            P("section", "expert", None, None),
        ),
        out_specs=P("section", None, "expert", None),
        check_vma=False,
    )
```
